32 devices in a mesh: groups: 2 (over x), row: 8 (over z, y), col: 2 (over core).
Axes of the slice: x: 2, y: 2, z: 4, core: 2. Of those that a mesh axis runs over, the one named last changes fastest.
Arguments:
- tokens_in: bfloat16 [16, 256, 768], P('groups', 'row'), parts along dimension 0, may hold values from -6 to 6
- cond_single: bfloat16 [512, 768], P(('groups', 'row')), parts along dimension 0, may hold values from -6 to 6
- token_mask: int32 [512], P(('groups', 'row')), parts along dimension 0, may hold values 0 or 1
- pair_cond: bfloat16 [512, 256, 128], P(('groups', 'row'), 'col'), parts along dimension 0, may hold values from -1000 to 1000
- w_pair: bfloat16 [128, 16], replicated, may hold values from -0.5 to 0.5
- w_scale: bfloat16 [768, 768], replicated, may hold values from -0.21875 to 0.21875
- w_shift: bfloat16 [768, 768], replicated, may hold values from -0.21875 to 0.21875
- w_outgate: bfloat16 [768, 768], replicated, may hold values from -0.21875 to 0.21875
- w_query: bfloat16 [768, 768], P(None, 'col'), may hold values from -0.21875 to 0.21875
- w_key: bfloat16 [768, 768], P(None, 'col'), may hold values from -0.21875 to 0.21875
- w_value: bfloat16 [768, 768], P(None, 'col'), may hold values from -0.21875 to 0.21875
- w_gate: bfloat16 [768, 768], P(None, 'col'), may hold values from -0.21875 to 0.21875
- w_out: bfloat16 [768, 768], P('col'), may hold values from -0.21875 to 0.21875
- atom_cond: bfloat16 [4096, 128], P(('groups', 'row', 'col')), parts along dimension 0, may hold values from -6 to 6
- atom_token: int32 [4096], P(('groups', 'row', 'col')), parts along dimension 0, may hold values from 0 to 255, as said below
- window_start: int32 [128], P(('groups', 'row', 'col')), parts along dimension 0, may hold values from 0 to 1920, as said below
- atom_mask: int32 [4096], P(('groups', 'row', 'col')), parts along dimension 0, may hold values 0 or 1
- atom_pair: bfloat16 [128, 16, 32, 128], P(('groups', 'row', 'col')), parts along dimension 0, may hold values from -1000 to 1000
- w_token_atom: bfloat16 [768, 128], replicated, may hold values from -0.21875 to 0.21875
- w_ascale: bfloat16 [128, 128], replicated, may hold values from -0.5 to 0.5
- w_ashift: bfloat16 [128, 128], replicated, may hold values from -0.5 to 0.5
- w_aquery: bfloat16 [128, 128], replicated, may hold values from -0.5 to 0.5
- w_akey: bfloat16 [128, 128], replicated, may hold values from -0.5 to 0.5
- w_avalue: bfloat16 [128, 128], replicated, may hold values from -0.5 to 0.5
- w_agate: bfloat16 [128, 128], replicated, may hold values from -0.5 to 0.5
- w_aout: bfloat16 [128, 128], replicated, may hold values from -0.5 to 0.5
- w_apair: bfloat16 [16, 4], replicated, may hold values from -1.5 to 1.5
- w_update: bfloat16 [3, 128], replicated, may hold values from -0.5 to 0.5
Outputs:
- tokens_out: bfloat16 [16, 256, 768], P('groups', 'row'), parts along dimension 0
- atom_update: float32 [16, 3, 2048], P('groups', None, ('row', 'col')), parts along dimension 0
The draws below stay inside these ranges and needn't reach their ends.
There are 2 independent parts, one for each index of `groups`. The reference program is written for one: setup_inputs(seed, part) draws one part's arguments, and reference() takes and returns one part's arrays. A program takes and returns all parts, laid end to end along the dimension named above; an argument that names none is the same for every part. Nothing has to cross between parts.
Inputs may be any that keep to these rules, and one draw needn't show every extreme that they name: atom_token[l] differs from l // 8 by at most 16. window_start[k] differs from k * 32 + 32 // 2 - 128 // 2 by at most 16, unless it is clipped to the range.
All inputs are finite; a program needn't handle non-finite values. No bound on the sum of `token_mask` or of `atom_mask` on one device may be relied on, other than what follows from the above.
Results may differ from the reference program's by a relative error of at most 0.0075.
Values may be sent and summed in bfloat16 or wider, within the bound.
A program may use at most 128 MiB of HBM per device.

```python
import jax
import jax.numpy as jnp
from jax import lax

D = 768
HEADS = 16
HEAD = 48
CZ = 128
DA = 128
AHEADS = 4
AHEAD = 32
CP = 16
WQ = 32
WK = 128
PER_TOKEN = 8
TOK_ROW = 32
SAMPLES = 8
TOKENS = 256
ATOMS = 2048
WINDOWS = 64


def draw_pair_cond(key, part):
    key_one = jax.random.fold_in(key, 0)
    normals = jax.random.normal(key_one, (TOKENS, TOKENS, CZ), jnp.float32)
    return jnp.clip(normals, -1000.0, 1000.0).astype(jnp.bfloat16)


def draw_atom_pair(key, part):
    key_one = jax.random.fold_in(key, 0)
    normals = jax.random.normal(key_one, (WINDOWS, CP, WQ, WK), jnp.float32)
    return jnp.clip(normals, -1000.0, 1000.0).astype(jnp.bfloat16)


def draw_atom_token(key, part):
    reach = TOK_ROW // 2
    position = jnp.arange(ATOMS, dtype=jnp.int32) // PER_TOKEN
    jitter = jax.random.randint(key, (ATOMS,), -reach, reach + 1, dtype=jnp.int32)
    token_ids = jnp.clip(position + jitter, 0, TOKENS - 1)
    middle = ATOMS // 2
    token_ids = token_ids.at[middle].set(middle // PER_TOKEN + reach)
    token_ids = token_ids.at[middle + 1].set((middle + 1) // PER_TOKEN - reach)
    token_ids = token_ids.at[0].set(0).at[ATOMS - 1].set(TOKENS - 1)
    return token_ids.astype(jnp.int32)


def draw_window_start(key, part):
    window_index = jnp.arange(WINDOWS, dtype=jnp.int32)
    jitter = jax.random.randint(key, (WINDOWS,), -(WQ // 2), WQ // 2 + 1, dtype=jnp.int32)
    return jnp.clip(window_index * WQ + WQ // 2 - WK // 2 + jitter, 0, ATOMS - WK).astype(jnp.int32)


def with_ends(drawn, stream_key, least, largest):
    longest = drawn.shape.index(max(drawn.shape))
    spots = []
    for shift in (0, 1):
        where = [jax.random.randint(jax.random.fold_in(stream_key, axis), (), 0, length) for axis, length in enumerate(drawn.shape)]
        where[longest] = (where[longest] + shift) % drawn.shape[longest]
        spots.append(tuple(where))
    return drawn.at[spots[0]].set(least).at[spots[1]].set(largest)


def level_of(stream_key, extent, cuts, smallest, top_value):
    factor_of, own = 1.0, jax.random.fold_in(stream_key, 6)
    for dim, shards_of in cuts:
        draws = jnp.exp(jax.random.uniform(jax.random.fold_in(own, dim), (shards_of,), jnp.float32, smallest / len(cuts), top_value / len(cuts)))
        factor_of = factor_of * jnp.repeat(draws, extent[dim] // shards_of).reshape([-1 if axis == dim else 1 for axis in range(len(extent))])
    return factor_of


def noise(own_key, dims, deviation, most, pieces=(), kind=jnp.bfloat16):
    drawn = deviation * jax.random.normal(own_key, dims, jnp.float32)
    if pieces:
        drawn = drawn * level_of(own_key, dims, pieces, -0.22, 0.18)
    return jnp.clip(drawn, -most, most).astype(kind)


def setup_inputs(seed: int = 0, part: int = 0) -> dict:
    keys = jax.random.split(jax.random.key(seed), 29)
    part_keys = jax.random.split(jax.random.fold_in(keys[28], part), 29)
    return {
        "tokens_in": noise(part_keys[0], (SAMPLES, TOKENS, D), 1.0, 6.0, ((1, 8),)),
        "cond_single": noise(part_keys[1], (TOKENS, D), 1.0, 6.0, ((0, 8),)),
        "token_mask": with_ends((jax.random.randint(part_keys[2], (TOKENS,), 0, 8) < 7).astype(jnp.int32), jax.random.fold_in(part_keys[2], 1), 0, 1),
        "pair_cond": draw_pair_cond(jax.random.fold_in(jax.random.fold_in(keys[28], part), 71), part),
        "w_pair": noise(keys[4], (CZ, HEADS), CZ ** -0.5, 0.5),
        "w_scale": noise(keys[5], (D, D), D ** -0.5, 0.21875),
        "w_shift": noise(keys[6], (D, D), D ** -0.5, 0.21875),
        "w_outgate": noise(keys[7], (D, D), D ** -0.5, 0.21875),
        "w_query": noise(keys[8], (D, D), D ** -0.5, 0.21875, ((1, 2),)),
        "w_key": noise(keys[9], (D, D), D ** -0.5, 0.21875, ((1, 2),)),
        "w_value": noise(keys[10], (D, D), D ** -0.5, 0.21875, ((1, 2),)),
        "w_gate": noise(keys[11], (D, D), D ** -0.5, 0.21875, ((1, 2),)),
        "w_out": noise(keys[12], (D, D), D ** -0.5, 0.21875, ((0, 2),)),
        "atom_cond": noise(part_keys[13], (ATOMS, DA), 1.0, 6.0, ((0, 16),)),
        "atom_token": draw_atom_token(jax.random.fold_in(jax.random.fold_in(keys[28], part), 71), part),
        "window_start": draw_window_start(jax.random.fold_in(jax.random.fold_in(keys[28], part), 71), part),
        "atom_mask": with_ends((jax.random.randint(part_keys[16], (ATOMS,), 0, 8) < 7).astype(jnp.int32), jax.random.fold_in(part_keys[16], 1), 0, 1),
        "atom_pair": draw_atom_pair(jax.random.fold_in(jax.random.fold_in(keys[28], part), 71), part),
        "w_token_atom": noise(keys[18], (D, DA), D ** -0.5, 0.21875),
        "w_ascale": noise(keys[19], (DA, DA), DA ** -0.5, 0.5),
        "w_ashift": noise(keys[20], (DA, DA), DA ** -0.5, 0.5),
        "w_aquery": noise(keys[21], (DA, DA), DA ** -0.5, 0.5),
        "w_akey": noise(keys[22], (DA, DA), DA ** -0.5, 0.5),
        "w_avalue": noise(keys[23], (DA, DA), DA ** -0.5, 0.5),
        "w_agate": noise(keys[24], (DA, DA), DA ** -0.5, 0.5),
        "w_aout": noise(keys[25], (DA, DA), DA ** -0.5, 0.5),
        "w_apair": noise(keys[26], (CP, AHEADS), CP ** -0.5, 1.5),
        "w_update": noise(keys[27], (3, DA), DA ** -0.5, 0.5),
    }


def layer_norm(inputs):
    inputs = inputs.astype(jnp.float32)
    centred = inputs - lax.optimization_barrier(jnp.mean(inputs, axis=-1, keepdims=True))
    variance = lax.optimization_barrier(jnp.mean(centred * centred, axis=-1, keepdims=True))
    return centred * lax.rsqrt(variance + 1e-05)

def rounded(inputs):
    return lax.optimization_barrier(inputs.astype(jnp.bfloat16)).astype(jnp.float32)

def reference(tokens_in, cond_single, token_mask, pair_cond, w_pair, w_scale, w_shift, w_outgate, w_query, w_key, w_value, w_gate, w_out, atom_cond, atom_token, window_start, atom_mask, atom_pair, w_token_atom, w_ascale, w_ashift, w_aquery, w_akey, w_avalue, w_agate, w_aout, w_apair, w_update):
    highest = lax.Precision.HIGHEST
    cond_norm = layer_norm(cond_single).astype(jnp.bfloat16)
    ada_scale = jax.nn.sigmoid(jnp.dot(cond_norm, w_scale, preferred_element_type=jnp.float32))
    ada_shift = jnp.dot(cond_norm, w_shift, preferred_element_type=jnp.float32)
    out_gate = jax.nn.sigmoid(jnp.dot(cond_norm, w_outgate, preferred_element_type=jnp.float32))
    pair_float = w_pair.astype(jnp.float32)
    pair_bias = lax.map(lambda pair_rows: jnp.dot(pair_rows.astype(jnp.float32), pair_float, precision=highest).T, pair_cond)
    mask_shift = (token_mask.astype(jnp.float32) - 1.0) * 10000.0
    inv_root = HEAD ** (-0.5)

    def token_sample(sample_rows):
        mixed_rows = (ada_scale * layer_norm(sample_rows) + ada_shift).astype(jnp.bfloat16)
        queries = (jnp.dot(mixed_rows, w_query, preferred_element_type=jnp.float32) * inv_root).astype(jnp.bfloat16).reshape(TOKENS, HEADS, HEAD)
        key_rows = jnp.dot(mixed_rows, w_key, preferred_element_type=jnp.float32).astype(jnp.bfloat16).reshape(TOKENS, HEADS, HEAD)
        value_rows = jnp.dot(mixed_rows, w_value, preferred_element_type=jnp.float32).astype(jnp.bfloat16).reshape(TOKENS, HEADS, HEAD)
        head_gate = jax.nn.sigmoid(jnp.dot(mixed_rows, w_gate, preferred_element_type=jnp.float32))
        scores = jnp.einsum('qhd,khd->qhk', queries.astype(jnp.float32), key_rows.astype(jnp.float32), precision=highest) + pair_bias + mask_shift
        row_max = lax.optimization_barrier(jnp.max(scores, axis=-1, keepdims=True))
        weights = jnp.exp(scores - row_max)
        totals = lax.optimization_barrier(jnp.sum(weights, axis=-1, keepdims=True))
        attended = jnp.einsum('qhk,khd->qhd', rounded(weights), value_rows.astype(jnp.float32), precision=highest) / totals
        gated = (head_gate * attended.reshape(TOKENS, D)).astype(jnp.bfloat16)
        update = jnp.dot(gated, w_out, preferred_element_type=jnp.float32)
        return (sample_rows.astype(jnp.float32) + out_gate * update).astype(jnp.bfloat16)
    tokens_out = lax.map(token_sample, tokens_in)

    def project_rows(sample_rows):
        token_norm = layer_norm(sample_rows).astype(jnp.bfloat16)
        return jnp.dot(token_norm, w_token_atom, preferred_element_type=jnp.float32).astype(jnp.bfloat16)
    token_proj = lax.map(project_rows, tokens_out)
    cond_anorm = layer_norm(atom_cond).astype(jnp.bfloat16)
    atom_scale = jax.nn.sigmoid(jnp.dot(cond_anorm, w_ascale, preferred_element_type=jnp.float32))
    atom_shift = jnp.dot(cond_anorm, w_ashift, preferred_element_type=jnp.float32)
    atom_bias = jnp.einsum('wcqk,ch->whqk', atom_pair.astype(jnp.float32), w_apair.astype(jnp.float32), precision=highest)
    key_index = window_start[:, None].astype(jnp.int32) + jnp.arange(WK, dtype=jnp.int32)[None, :]
    atom_root = AHEAD ** (-0.5)
    live = atom_mask.astype(jnp.float32)

    def atom_sample(projected):
        atom_state = atom_cond.astype(jnp.float32) + projected[atom_token].astype(jnp.float32)
        atom_mixed = (atom_scale * layer_norm(atom_state) + atom_shift).astype(jnp.bfloat16)
        queries = (jnp.dot(atom_mixed, w_aquery, preferred_element_type=jnp.float32) * atom_root).astype(jnp.bfloat16).reshape(WINDOWS, WQ, AHEADS, AHEAD)
        key_rows = jnp.dot(atom_mixed, w_akey, preferred_element_type=jnp.float32).astype(jnp.bfloat16).reshape(ATOMS, AHEADS, AHEAD)[key_index]
        value_rows = jnp.dot(atom_mixed, w_avalue, preferred_element_type=jnp.float32).astype(jnp.bfloat16).reshape(ATOMS, AHEADS, AHEAD)[key_index]
        atom_gate = jax.nn.sigmoid(jnp.dot(atom_mixed, w_agate, preferred_element_type=jnp.float32))
        scores = jnp.einsum('wqhd,wkhd->whqk', queries.astype(jnp.float32), key_rows.astype(jnp.float32), precision=highest) + atom_bias
        row_max = lax.optimization_barrier(jnp.max(scores, axis=-1, keepdims=True))
        weights = jnp.exp(scores - row_max)
        totals = lax.optimization_barrier(jnp.sum(weights, axis=-1, keepdims=True))
        attended = jnp.einsum('whqk,wkhd->wqhd', rounded(weights), value_rows.astype(jnp.float32), precision=highest) / jnp.transpose(totals, (0, 2, 1, 3))
        gated = (atom_gate * attended.reshape(ATOMS, DA)).astype(jnp.bfloat16)
        atom_final = atom_state + jnp.dot(gated, w_aout, preferred_element_type=jnp.float32)
        final_norm = layer_norm(atom_final).astype(jnp.bfloat16)
        return jnp.dot(w_update, final_norm.T, preferred_element_type=jnp.float32) * live[None, :]
    atom_update = lax.map(atom_sample, token_proj)
    return (tokens_out, atom_update)
```

```python
import functools

import jax
import jax.numpy as jnp
from jax import lax
from jax.experimental import pallas as pl
from jax.experimental.pallas import tpu as pltpu
from jax.sharding import PartitionSpec as P

HEAD = 48
AHEADS = 4
AHEAD = 32
WQ = 32
WK = 128
CHUNKS = 2
F32 = jnp.float32
BF16 = jnp.bfloat16


def layer_norm(inputs):
    inputs = inputs.astype(F32)
    centred = inputs - jnp.mean(inputs, axis=-1, keepdims=True)
    variance = jnp.mean(centred * centred, axis=-1, keepdims=True)
    return centred * lax.rsqrt(variance + 1e-05)


def dot(a, b):
    return jnp.dot(a, b, preferred_element_type=F32)


def dot_nt(a, b):
    return lax.dot_general(a, b, (((1,), (1,)), ((), ())), preferred_element_type=F32)


def remote(src, dst, send, recv, row, col):
    return pltpu.make_async_remote_copy(
        src_ref=src,
        dst_ref=dst,
        send_sem=send,
        recv_sem=recv,
        device_id={"row": row, "col": col},
        device_id_type=pl.DeviceIdType.MESH,
    )


def token_kernel(
    rows,
    tin, cond, tmask, pc, wpt, wsc, wsh, wog, wq, wk, wv, wg, wo, wta, acond, atok,
    tout, lk_out, ac_out, tk_out,
    mx, qb, gate, og, gated, gsib, wosib, pbs, bias, bfull, mk, lk, ac, tk,
    zs, zr, ys, yr, cs, cr, ms, mr, gs, gr, xs, xr,
):
    r = lax.axis_index("row")
    c = lax.axis_index("col")
    other = 1 - c
    samples, toks, width = tin.shape
    heads = wpt.shape[0] // 2
    half = pc.shape[1]
    total = half * 2
    n = rows // 2
    i = r // 2
    y = r % 2
    hs = samples // 2
    ns = hs // CHUNKS
    inv_root = HEAD ** (-0.5)

    def wrap(v):
        return lax.rem(v + rows, rows)

    left_row, right_row = wrap(r + c - 1), wrap(r + c)

    barrier = pltpu.get_barrier_semaphore()

    def greet(row, col):
        pl.semaphore_signal(
            barrier, inc=1, device_id={"row": row, "col": col},
            device_id_type=pl.DeviceIdType.MESH,
        )

    for d in range(1, rows):
        greet(wrap(r + d), c)
    greet(r, other)
    greet(wrap(r + 2 * c - 1), other)
    pl.semaphore_wait(barrier, rows + 1)

    cond_norm = layer_norm(cond[...]).astype(BF16)
    scale = jax.nn.sigmoid(dot(cond_norm, wsc[...]))
    shift = dot(cond_norm, wsh[...])
    for s in range(samples):
        mx[r, s] = (scale * layer_norm(tin[s]) + shift).astype(BF16)

    started = []

    def go(copy):
        copy.start()
        started.append(copy)
        return copy

    def block(row, core, j):
        return mx.at[row, pl.ds(core * hs + j * ns, ns)]

    def z_row(d):
        return lax.rem(i + n + d, n) * 2 + y

    for j in range(CHUNKS):
        own = block(r, c, j)
        for d in range(1, n):
            go(remote(own, own, zs.at[j, d - 1], zr.at[j, d - 1], z_row(d), c))
        go(remote(own, own, ys.at[j, 0], yr.at[j, 0], i * 2 + 1 - y, c))

    placed = (
        lax.broadcasted_iota(jnp.int32, (toks, total), 1)
        == lax.broadcasted_iota(jnp.int32, (toks, total), 0) + r * toks
    ).astype(F32)
    valid = jnp.broadcast_to(tmask[...], (8, toks)).astype(F32)
    mk[r] = dot(valid, placed)
    mask_copies = [
        go(remote(mk.at[r], mk.at[r], ms.at[d - 1], mr.at[d - 1], wrap(r + d), c))
        for d in range(1, rows)
    ]
    tk[1] = jnp.broadcast_to(atok[...], (8, atok.shape[1])).astype(F32)
    edge = WK // 2
    atoms = acond.shape[0]
    ac[edge : edge + atoms] = acond[...]
    wide = [
        go(remote(wo, wosib, xs.at[0], xr.at[0], r, other)),
        go(remote(tk.at[1], tk.at[0], xs.at[1], xr.at[1], right_row, other)),
        go(remote(tk.at[1], tk.at[2], xs.at[2], xr.at[2], left_row, other)),
        go(remote(ac.at[pl.ds(atoms, edge)], ac.at[pl.ds(0, edge)], xs.at[3], xr.at[3], right_row, other)),
        go(remote(ac.at[pl.ds(edge, edge)], ac.at[pl.ds(atoms + edge, edge)], xs.at[4], xr.at[4], left_row, other)),
    ]

    for q in range(toks):
        part = dot_nt(wpt[...], pc[q])
        pbs[0, q * heads : (q + 1) * heads] = part[:heads]
        pbs[1, q * heads : (q + 1) * heads] = part[heads:]
    bias_copy = go(remote(pbs.at[other], bias.at[c], xs.at[5], xr.at[5], r, other))
    bias[c] = pbs[c]

    own_rows = mx[r].reshape(samples * toks, width)
    qb[...] = (dot(own_rows, wq[...]) * inv_root).astype(BF16).astype(F32).reshape(qb.shape)
    gate[...] = jax.nn.sigmoid(dot(own_rows, wg[...])).reshape(gate.shape)
    og[...] = jax.nn.sigmoid(dot(cond_norm, wog[...]))

    def forward_z(j, d):
        src = z_row(-d)
        got = block(src, c, j)
        remote(got, got, zs.at[j, d - 1], zr.at[j, d - 1], src, c).wait_recv()
        go(remote(got, got, ys.at[j, d], yr.at[j, d], i * 2 + 1 - y, c))
        go(remote(got, got, cs.at[j, d - 1], cr.at[j, d - 1], r, other))

    def forward_y(j, d):
        src = lax.rem(i + n - d, n) * 2 + 1 - y
        got = block(src, c, j)
        remote(got, got, ys.at[j, d], yr.at[j, d], i * 2 + 1 - y, c).wait_recv()
        go(remote(got, got, cs.at[j, n - 1 + d], cr.at[j, n - 1 + d], r, other))

    def arrived(j):
        for d in range(1, n):
            got = block(z_row(-d), other, j)
            remote(got, got, cs.at[j, d - 1], cr.at[j, d - 1], r, other).wait_recv()
        for d in range(n):
            got = block(lax.rem(i + n - d, n) * 2 + 1 - y, other, j)
            remote(got, got, cs.at[j, n - 1 + d], cr.at[j, n - 1 + d], r, other).wait_recv()

    columns = wq.shape[1]
    lane = lax.broadcasted_iota(jnp.int32, (heads, columns), 1)
    first = lax.broadcasted_iota(jnp.int32, (heads, columns), 0) * HEAD
    head_mask = ((lane >= first) & (lane < first + HEAD)).astype(F32)

    def attend(s, carry):
        keys_in = mx[:, s].reshape(total, width)
        keys = dot(keys_in, wk[...]).astype(BF16)
        values = dot(keys_in, wv[...]).astype(BF16)
        wide_q = (qb[s][:, None, :] * head_mask[None]).reshape(toks * heads, columns).astype(BF16)
        scores = dot_nt(wide_q, keys) + bfull[...]
        weights = jnp.exp(scores - jnp.max(scores, axis=-1, keepdims=True))
        totals = jnp.sum(weights, axis=-1, keepdims=True)
        summed = dot(weights.astype(BF16), values) / totals
        picked = summed.reshape(toks, heads, columns) * head_mask[None]
        gated[s] = (gate[s] * jnp.sum(picked, axis=1)).astype(BF16)
        return carry

    for d in range(1, n):
        forward_z(0, d)
    for d in range(n):
        forward_y(0, d)
    for d in range(1, rows):
        slot = mk.at[wrap(r - d)]
        remote(slot, slot, ms.at[d - 1], mr.at[d - 1], r, c).wait_recv()
    got_bias = bias.at[other]
    remote(pbs.at[other], got_bias, xs.at[5], xr.at[5], r, other).wait_recv()
    shift_row = (jnp.sum(mk[...], axis=0) - 1.0)[0:1] * 10000.0
    for k in range(2):
        cut = slice(k * half, (k + 1) * half)
        bfull[:, cut] = bias[k] + shift_row[:, cut]
    gated_copies = []
    for j in range(CHUNKS):
        arrived(j)
        for part in range(2):
            base = part * hs + j * ns
            if j + 1 < CHUNKS:
                for d in range(1, n):
                    if (d - 1) * 2 // max(n - 1, 1) == part:
                        forward_z(j + 1, d)
            lax.fori_loop(base, base + ns, attend, None)
            k = j * 2 + part
            piece = pl.ds(base, ns)
            gated_copies.append(
                go(remote(gated.at[piece], gsib.at[piece], gs.at[k], gr.at[k], r, other))
            )
        if j + 1 < CHUNKS:
            for d in range(n):
                forward_y(j + 1, d)

    wide[0].wait_recv()
    own_part = dot(gated[...].reshape(samples * toks, columns), wo[...])
    for copy in gated_copies:
        copy.wait_recv()
    update = own_part + dot(gsib[...].reshape(samples * toks, columns), wosib[...])
    for s in range(samples):
        tokens = (tin[s].astype(F32) + og[...] * update[s * toks : (s + 1) * toks]).astype(BF16)
        tout[s] = tokens
        proj = dot(layer_norm(tokens).astype(BF16), wta[...]).astype(BF16)
        lk[toks : 2 * toks, s * proj.shape[1] : (s + 1) * proj.shape[1]] = proj
    mine = lk.at[pl.ds(toks, toks)]
    near = [
        go(remote(mine, lk.at[pl.ds(0, toks)], xs.at[6], xr.at[6], wrap(r + 1), c)),
        go(remote(mine, lk.at[pl.ds(2 * toks, toks)], xs.at[7], xr.at[7], wrap(r - 1), c)),
    ]
    for copy in wide[1:] + near:
        copy.wait_recv()
    lk_out[...] = lk[...]
    ac_out[...] = ac[...]
    tk_out[...] = tk[...]
    for copy in started:
        copy.wait_send()


def atom_kernel(
    lk, ac, tk, start, wap, amask, apair, wasc, wash, waq, wak, wav, wag, wao, wup, out
):
    r = lax.axis_index("row")
    c = lax.axis_index("col")
    samples = out.shape[0]
    atoms = amask.shape[1]
    da = ac.shape[1]
    span = ac.shape[0]
    edge = WK // 2
    windows = atoms // WQ
    near = lk.shape[0]
    toks = near // 3
    cond = ac[...].astype(F32)
    cond_norm = layer_norm(cond).astype(BF16)
    scale = jax.nn.sigmoid(dot(cond_norm, wasc[...]))
    shift = dot(cond_norm, wash[...])
    cols = [jnp.transpose(tk[k])[:, 0:1] for k in range(3)]
    token = jnp.concatenate([cols[0][atoms - edge :], cols[1], cols[2][:edge]], axis=0)
    token = token - (r * toks - toks).astype(F32)
    pick = (token == lax.broadcasted_iota(jnp.int32, (span, near), 1).astype(F32)).astype(BF16)
    looked = dot(pick, lk[...])

    base = (r * 2 + c) * atoms - edge
    place = lax.broadcasted_iota(jnp.int32, (WK, span), 1) - lax.broadcasted_iota(
        jnp.int32, (WK, span), 0
    )
    windowed = jnp.concatenate(
        [(place == start[w] - base).astype(F32) for w in range(windows)], axis=0
    ).astype(BF16)

    biases = []
    for w in range(windows):
        per_head = [None] * AHEADS
        for ch in range(apair.shape[1]):
            plane = apair[w, ch].astype(F32)
            for h in range(AHEADS):
                term = plane * wap[ch * AHEADS + h]
                per_head[h] = term if ch == 0 else per_head[h] + term
        biases.append(jnp.concatenate(per_head, axis=0))

    lane = lax.broadcasted_iota(jnp.int32, (1, da), 1)
    masks = [((lane >= h * AHEAD) & (lane < (h + 1) * AHEAD)).astype(F32) for h in range(AHEADS)]
    w_kv = jnp.concatenate([wak[...], wav[...]], axis=1)
    w_qg = jnp.concatenate([waq[...], wag[...]], axis=1)
    root = AHEAD ** (-0.5)
    live = amask[...].astype(F32)
    for s in range(samples):
        state = cond + looked[:, s * da : (s + 1) * da]
        mixed = (scale * layer_norm(state) + shift).astype(BF16)
        kv = dot(mixed, w_kv).astype(BF16)
        own = dot(mixed[edge : edge + atoms], w_qg)
        queries = (own[:, :da] * root).astype(BF16).astype(F32)
        gate = jax.nn.sigmoid(own[:, da:])
        wkv = dot(windowed, kv).astype(BF16)
        parts = []
        for w in range(windows):
            q = queries[w * WQ : (w + 1) * WQ]
            wide_q = jnp.concatenate([q * m for m in masks], axis=0).astype(BF16)
            here = wkv[w * WK : (w + 1) * WK]
            scores = dot_nt(wide_q, here[:, :da]) + biases[w]
            weights = jnp.exp(scores - jnp.max(scores, axis=-1, keepdims=True))
            totals = jnp.sum(weights, axis=-1, keepdims=True)
            summed = dot(weights.astype(BF16), here[:, da:]) / totals
            picked = summed[:WQ] * masks[0]
            for h in range(1, AHEADS):
                picked = picked + summed[h * WQ : (h + 1) * WQ] * masks[h]
            parts.append(picked)
        gated = (gate * jnp.concatenate(parts, axis=0)).astype(BF16)
        final = state[edge : edge + atoms] + dot(gated, wao[...])
        out[s] = dot_nt(wup[...], layer_norm(final).astype(BF16)) * live


def shards(
    rows,
    tokens_in, cond_single, token_mask, pair_cond, w_pair, w_scale, w_shift, w_outgate,
    w_query, w_key, w_value, w_gate, w_out, atom_cond, atom_token, window_start, atom_mask,
    atom_pair, w_token_atom, w_ascale, w_ashift, w_aquery, w_akey, w_avalue, w_agate, w_aout,
    w_apair, w_update,
):
    samples, toks, width = tokens_in.shape
    half = pair_cond.shape[1]
    total = 2 * half
    heads = w_pair.shape[1] // 2
    columns = w_query.shape[1]
    atoms, da = atom_cond.shape
    n = rows // 2
    vmem = pl.BlockSpec(memory_space=pltpu.VMEM)
    smem = pl.BlockSpec(memory_space=pltpu.SMEM)
    dma = pltpu.SemaphoreType.DMA
    flat = samples * toks
    flops = 2 * samples * total * width * columns * 4
    tokens_out, lookup, atoms_near, tokens_near = pl.pallas_call(
        functools.partial(token_kernel, rows),
        name="token_step",
        out_shape=(
            jax.ShapeDtypeStruct((samples, toks, width), BF16),
            jax.ShapeDtypeStruct((3 * toks, samples * da), BF16),
            jax.ShapeDtypeStruct((atoms + WK, da), BF16),
            jax.ShapeDtypeStruct((3, 8, atoms), F32),
        ),
        in_specs=[vmem] * 16,
        out_specs=[vmem] * 4,
        scratch_shapes=[
            pltpu.VMEM((rows, samples, toks, width), BF16),
            pltpu.VMEM((samples, toks, columns), F32),
            pltpu.VMEM((samples, toks, columns), F32),
            pltpu.VMEM((toks, width), F32),
            pltpu.VMEM((samples, toks, columns), BF16),
            pltpu.VMEM((samples, toks, columns), BF16),
            pltpu.VMEM((columns, width), BF16),
            pltpu.VMEM((2, toks * heads, half), F32),
            pltpu.VMEM((2, toks * heads, half), F32),
            pltpu.VMEM((toks * heads, total), F32),
            pltpu.VMEM((rows, 8, total), F32),
            pltpu.VMEM((3 * toks, samples * da), BF16),
            pltpu.VMEM((atoms + WK, da), BF16),
            pltpu.VMEM((3, 8, atoms), F32),
            dma((CHUNKS, n - 1)),
            dma((CHUNKS, n - 1)),
            dma((CHUNKS, n)),
            dma((CHUNKS, n)),
            dma((CHUNKS, rows - 1)),
            dma((CHUNKS, rows - 1)),
            dma((rows - 1,)),
            dma((rows - 1,)),
            dma((2 * CHUNKS,)),
            dma((2 * CHUNKS,)),
            dma((8,)),
            dma((8,)),
        ],
        compiler_params=pltpu.CompilerParams(
            collective_id=0, has_side_effects=True, vmem_limit_bytes=56 * 2**20
        ),
        cost_estimate=pl.CostEstimate(
            flops=flops, bytes_accessed=12 * 2**20, transcendentals=flat * total * heads
        ),
    )(
        tokens_in, cond_single, token_mask.reshape(1, toks), pair_cond, w_pair.T, w_scale, w_shift,
        w_outgate, w_query, w_key, w_value, w_gate, w_out, w_token_atom, atom_cond,
        atom_token.reshape(1, atoms),
    )
    atom_update = pl.pallas_call(
        atom_kernel,
        name="atom_step",
        out_shape=jax.ShapeDtypeStruct((samples, 3, atoms), F32),
        in_specs=[vmem] * 3 + [smem] * 2 + [vmem] * 10,
        out_specs=vmem,
        compiler_params=pltpu.CompilerParams(vmem_limit_bytes=32 * 2**20),
        cost_estimate=pl.CostEstimate(
            flops=2 * samples * atoms * da * 3000, bytes_accessed=2**20, transcendentals=2**19
        ),
    )(
        lookup, atoms_near, tokens_near, window_start, w_apair.astype(F32).reshape(-1),
        atom_mask.reshape(1, atoms), atom_pair, w_ascale, w_ashift, w_aquery, w_akey, w_avalue,
        w_agate, w_aout, w_update,
    )
    return (tokens_out, atom_update)


def solution(mesh):
    return jax.shard_map(
        functools.partial(shards, mesh.shape["row"]),
        mesh=mesh,
        in_specs=(
            P("groups", "row", None),
            P(("groups", "row"), None),
            P(("groups", "row")),
            P(("groups", "row"), "col", None),
            P(),
            P(),
            P(),
            P(),
            P(None, "col"),
            P(None, "col"),
            P(None, "col"),
            P(None, "col"),
            P("col", None),
            P(("groups", "row", "col"), None),
            P(("groups", "row", "col")),
            P(("groups", "row", "col")),
            P(("groups", "row", "col")),
            P(("groups", "row", "col"), None, None, None),
            P(),
            P(),
            P(),
            P(),
            P(),
            P(),
            P(),
            P(),
            P(),
            P(),
        ),
        out_specs=(P("groups", "row", None), P("groups", None, ("row", "col"))),
        check_vma=False,
    )
```

```python
import functools

import jax
import jax.numpy as jnp
from jax import lax
from jax.experimental import pallas as pl
from jax.experimental.pallas import tpu as pltpu
from jax.sharding import PartitionSpec as P

HEAD = 48
AHEADS = 4
AHEAD = 32
WQ = 32
WK = 128
CHUNKS = 2
F32 = jnp.float32
BF16 = jnp.bfloat16


def layer_norm(inputs):
    inputs = inputs.astype(F32)
    centred = inputs - jnp.mean(inputs, axis=-1, keepdims=True)
    variance = jnp.mean(centred * centred, axis=-1, keepdims=True)
    return centred * lax.rsqrt(variance + 1e-05)


def dot(a, b):
    return jnp.dot(a, b, preferred_element_type=F32)


def dot_nt(a, b):
    return lax.dot_general(a, b, (((1,), (1,)), ((), ())), preferred_element_type=F32)


def remote(src, dst, send, recv, row, col):
    return pltpu.make_async_remote_copy(
        src_ref=src,
        dst_ref=dst,
        send_sem=send,
        recv_sem=recv,
        device_id={"row": row, "col": col},
        device_id_type=pl.DeviceIdType.MESH,
    )


def step_kernel(
    rows,
    cond, tmask, wpt, acond, atok, amask, start, wap, wasc, wash, waq, wak, wav, wag, wao, wup,
    tin_h, wsc_h, wsh_h, pc_h, wq_h, wg_h, wo_h, wog_h, wk_h, wv_h, wta_h, apair_h,
    tout, out,
    tin, wsc, wsh, pc, wq, wg, wo, wog, wk, wv, wta, apair,
    mx, qb, gate, og, gated, gsib, wosib, pbs, bias, bfull, mk, lk, ac, tk,
    asc, ash, pick, windowed, abias,
    ls, zs, zr, ys, yr, cs, cr, ms, mr, gs, gr, xs, xr,
):
    r = lax.axis_index("row")
    c = lax.axis_index("col")
    other = 1 - c
    samples, toks, width = tin.shape
    heads = wpt.shape[0] // 2
    half = pc.shape[1]
    total = half * 2
    n = rows // 2
    i = r // 2
    y = r % 2
    hs = samples // 2
    ns = hs // CHUNKS
    inv_root = HEAD ** (-0.5)

    def wrap(v):
        return lax.rem(v + rows, rows)

    left_row, right_row = wrap(r + c - 1), wrap(r + c)

    pairs = [
        (tin_h, tin), (wsc_h, wsc), (wsh_h, wsh), (pc_h, pc), (wq_h, wq), (wg_h, wg), (wo_h, wo),
        (wog_h, wog), (wk_h, wk), (wv_h, wv), (wta_h, wta), (apair_h, apair),
    ]
    loads = [pltpu.make_async_copy(src, dst, ls.at[k]) for k, (src, dst) in enumerate(pairs)]
    for load in loads[:3]:
        load.start()

    barrier = pltpu.get_barrier_semaphore()

    def greet(row, col):
        pl.semaphore_signal(
            barrier, inc=1, device_id={"row": row, "col": col},
            device_id_type=pl.DeviceIdType.MESH,
        )

    for d in range(1, rows):
        greet(wrap(r + d), c)
    greet(r, other)
    greet(wrap(r + 2 * c - 1), other)

    cond_norm = layer_norm(cond[...]).astype(BF16)
    for load in loads[:3]:
        load.wait()
    for load in loads[3:]:
        load.start()
    scale = jax.nn.sigmoid(dot(cond_norm, wsc[...]))
    shift = dot(cond_norm, wsh[...])
    for s in range(samples):
        mx[r, s] = (scale * layer_norm(tin[s]) + shift).astype(BF16)
    pl.semaphore_wait(barrier, rows + 1)

    started = []

    def go(copy):
        copy.start()
        started.append(copy)
        return copy

    def block(row, core, j):
        return mx.at[row, pl.ds(core * hs + j * ns, ns)]

    steps = [(t, way) for t in range(1, n) for way in (0, 1)]
    ids = {step: k for k, step in enumerate(steps)}
    partner = i * 2 + 1 - y

    def valid(step):
        t, way = step
        return i >= t if way == 0 else i + t < n

    def line(step):
        t, way = step
        return lax.rem(i + n - t, n) if way == 0 else lax.rem(i + t, n)

    def z_copy(j, step):
        t, way = step
        back = t - 1
        src = lax.rem(i + n - back, n) if way == 0 else lax.rem(i + back, n)
        dest = lax.rem(i + 1, n) if way == 0 else lax.rem(i + n - 1, n)
        ref = block(src * 2 + y, c, j)
        k = ids[step]
        return remote(ref, ref, zs.at[j, k], zr.at[j, k], dest * 2 + y, c)

    def z_sends(step):
        t, way = step
        if way == 0:
            return (i + 1 < n) & (i + 1 >= t)
        return (i >= 1) & (i + t <= n)

    def y_copy(j, k):
        src = i if k == 0 else line(steps[k - 1])
        ref = block(src * 2 + y, c, j)
        return remote(ref, ref, ys.at[j, k], yr.at[j, k], partner, c)

    def c_copy(j, k, over_y, core):
        src = i if k == 0 else line(steps[k - 1])
        col = 1 - y if over_y else y
        ref = block(src * 2 + col, core, j)
        slot = len(steps) + k if over_y else k - 1
        return remote(ref, ref, cs.at[j, slot], cr.at[j, slot], r, other)

    def y_arriving(j, k):
        src = i if k == 0 else line(steps[k - 1])
        ref = block(src * 2 + 1 - y, c, j)
        return remote(ref, ref, ys.at[j, k], yr.at[j, k], partner, c)

    def z_arriving(j, step):
        ref = block(line(step) * 2 + y, c, j)
        k = ids[step]
        return remote(ref, ref, zs.at[j, k], zr.at[j, k], r, other)

    def send_own(j):
        for way in (0, 1):
            pl.when(z_sends((1, way)))(lambda: z_copy(j, (1, way)).start())
        y_copy(j, 0).start()

    def forward_z(j, t):
        for way in (0, 1):
            step = (t, way)

            @pl.when(valid(step))
            def _():
                z_arriving(j, step).wait_recv()
                if t + 1 < n:
                    pl.when(z_sends((t + 1, way)))(lambda: z_copy(j, (t + 1, way)).start())
                y_copy(j, ids[step] + 1).start()
                c_copy(j, ids[step] + 1, False, c).start()

    def forward_y(j, t):
        if t == 0:
            y_arriving(j, 0).wait_recv()
            c_copy(j, 0, True, c).start()
            return
        for way in (0, 1):
            step = (t, way)

            @pl.when(valid(step))
            def _():
                y_arriving(j, ids[step] + 1).wait_recv()
                c_copy(j, ids[step] + 1, True, c).start()

    def arrived(j):
        c_copy(j, 0, True, other).wait_recv()
        for step in steps:

            @pl.when(valid(step))
            def _():
                c_copy(j, ids[step] + 1, False, other).wait_recv()
                c_copy(j, ids[step] + 1, True, other).wait_recv()

    def all_sent(j):
        y_copy(j, 0).wait_send()
        c_copy(j, 0, True, c).wait_send()
        for step in steps:
            pl.when(z_sends(step))(lambda: z_copy(j, step).wait_send())

            @pl.when(valid(step))
            def _():
                y_copy(j, ids[step] + 1).wait_send()
                c_copy(j, ids[step] + 1, False, c).wait_send()
                c_copy(j, ids[step] + 1, True, c).wait_send()

    send_own(0)

    placed = (
        lax.broadcasted_iota(jnp.int32, (toks, total), 1)
        == lax.broadcasted_iota(jnp.int32, (toks, total), 0) + r * toks
    ).astype(F32)
    present = jnp.broadcast_to(tmask[...], (8, toks)).astype(F32)
    mk[r] = dot(present, placed)
    for d in range(1, rows):
        go(remote(mk.at[r], mk.at[r], ms.at[d - 1], mr.at[d - 1], wrap(r + d), c))
    tk[1] = jnp.broadcast_to(atok[...], (8, atok.shape[1])).astype(F32)
    edge = WK // 2
    atoms = acond.shape[0]
    ac[edge : edge + atoms] = acond[...]
    edges = [
        go(remote(tk.at[1], tk.at[0], xs.at[1], xr.at[1], right_row, other)),
        go(remote(tk.at[1], tk.at[2], xs.at[2], xr.at[2], left_row, other)),
        go(remote(ac.at[pl.ds(atoms, edge)], ac.at[pl.ds(0, edge)], xs.at[3], xr.at[3], right_row, other)),
        go(remote(ac.at[pl.ds(edge, edge)], ac.at[pl.ds(atoms + edge, edge)], xs.at[4], xr.at[4], left_row, other)),
    ]

    loads[3].wait()
    for q in range(toks):
        part = dot_nt(wpt[...], pc[q])
        pbs[0, q * heads : (q + 1) * heads] = part[:heads]
        pbs[1, q * heads : (q + 1) * heads] = part[heads:]
    bias_copy = go(remote(pbs.at[other], bias.at[c], xs.at[5], xr.at[5], r, other))
    bias[c] = pbs[c]
    forward_z(0, 1)
    forward_y(0, 0)
    send_own(1)

    for load in loads[4:7]:
        load.wait()
    wide_out = go(remote(wo, wosib, xs.at[0], xr.at[0], r, other))
    own_rows = mx[r].reshape(samples * toks, width)
    qb[...] = (dot(own_rows, wq[...]) * inv_root).astype(BF16).astype(F32).reshape(qb.shape)
    gate[...] = jax.nn.sigmoid(dot(own_rows, wg[...])).reshape(gate.shape)
    forward_z(0, 2)
    forward_y(0, 1)
    loads[7].wait()
    og[...] = jax.nn.sigmoid(dot(cond_norm, wog[...]))

    for copy in edges:
        copy.wait_recv()
    da = ac.shape[1]
    span = ac.shape[0]
    windows = atoms // WQ
    near = lk.shape[0]
    atom_cond = ac[...].astype(F32)
    atom_norm = layer_norm(atom_cond).astype(BF16)
    asc[...] = jax.nn.sigmoid(dot(atom_norm, wasc[...]))
    ash[...] = dot(atom_norm, wash[...])
    cols = [jnp.transpose(tk[k])[:, 0:1] for k in range(3)]
    token = jnp.concatenate([cols[0][atoms - edge :], cols[1], cols[2][:edge]], axis=0)
    token = token - (r * toks - toks).astype(F32)
    pick[...] = (
        token == lax.broadcasted_iota(jnp.int32, (span, near), 1).astype(F32)
    ).astype(BF16)
    base = (r * 2 + c) * atoms - edge
    place = lax.broadcasted_iota(jnp.int32, (WK, span), 1) - lax.broadcasted_iota(
        jnp.int32, (WK, span), 0
    )
    for w in range(windows):
        windowed[w * WK : (w + 1) * WK] = (place == start[w] - base).astype(F32).astype(BF16)
    for t in range(3, n):
        forward_z(0, t)
    loads[11].wait()
    for h in range(AHEADS):
        acc = apair[:, 0].astype(F32) * wap[h]
        for ch in range(1, apair.shape[1]):
            acc = acc + apair[:, ch].astype(F32) * wap[ch * AHEADS + h]
        abias[:, h * WQ : (h + 1) * WQ] = acc
    for t in range(2, n):
        forward_y(0, t)

    columns = wq.shape[1]
    lane = lax.broadcasted_iota(jnp.int32, (heads, columns), 1)
    first = lax.broadcasted_iota(jnp.int32, (heads, columns), 0) * HEAD
    head_mask = ((lane >= first) & (lane < first + HEAD)).astype(F32)

    def attend(s, carry):
        keys_in = mx[:, s].reshape(total, width)
        keys = dot(keys_in, wk[...]).astype(BF16)
        values = dot(keys_in, wv[...]).astype(BF16)
        values = jnp.concatenate([values, jnp.ones((total, 128), BF16)], axis=1)
        wide_q = (qb[s][:, None, :] * head_mask[None]).reshape(toks * heads, columns).astype(BF16)
        scores = dot_nt(wide_q, keys) + bfull[...]
        weights = jnp.exp(scores - jnp.max(scores, axis=-1, keepdims=True))
        summed = dot(weights.astype(BF16), values)
        inverse = 1.0 / summed[:, columns:]
        summed = summed[:, :columns] * jnp.concatenate([inverse] * (columns // 128), axis=1)
        picked = summed.reshape(toks, heads, columns) * head_mask[None]
        gated[s] = (gate[s] * jnp.sum(picked, axis=1)).astype(BF16)
        return carry

    for d in range(1, rows):
        slot = mk.at[wrap(r - d)]
        remote(slot, slot, ms.at[d - 1], mr.at[d - 1], r, other).wait_recv()
    bias_copy.wait_recv()
    shift_row = (jnp.sum(mk[...], axis=0) - 1.0)[0:1] * 10000.0
    for k in range(2):
        cut = slice(k * half, (k + 1) * half)
        bfull[:, cut] = bias[k] + shift_row[:, cut]
    loads[8].wait()
    loads[9].wait()
    gated_copies = []

    def send_gated(j, part):
        piece = pl.ds(part * hs + j * ns, ns)
        k = j * 2 + part
        gated_copies.append(
            go(remote(gated.at[piece], gsib.at[piece], gs.at[k], gr.at[k], r, other))
        )

    forward_z(1, 1)
    forward_y(1, 0)
    arrived(0)
    lax.fori_loop(0, ns, attend, None)
    send_gated(0, 0)
    forward_z(1, 2)
    forward_y(1, 1)
    lax.fori_loop(hs, hs + ns, attend, None)
    send_gated(0, 1)
    for t in range(3, n):
        forward_z(1, t)
    for t in range(2, n):
        forward_y(1, t)
    arrived(1)
    lax.fori_loop(ns, 2 * ns, attend, None)
    send_gated(1, 0)
    lax.fori_loop(hs + ns, hs + 2 * ns, attend, None)
    send_gated(1, 1)

    wide_out.wait_recv()
    own_part = dot(gated[...].reshape(samples * toks, columns), wo[...])
    loads[10].wait()
    for copy in gated_copies:
        copy.wait_recv()
    update = own_part + dot(gsib[...].reshape(samples * toks, columns), wosib[...])
    for s in range(samples):
        tokens = (tin[s].astype(F32) + og[...] * update[s * toks : (s + 1) * toks]).astype(BF16)
        tout[s] = tokens
        proj = dot(layer_norm(tokens).astype(BF16), wta[...]).astype(BF16)
        lk[toks : 2 * toks, s * da : (s + 1) * da] = proj
    mine = lk.at[pl.ds(toks, toks)]
    around = [
        go(remote(mine, lk.at[pl.ds(0, toks)], xs.at[6], xr.at[6], wrap(r + 1), c)),
        go(remote(mine, lk.at[pl.ds(2 * toks, toks)], xs.at[7], xr.at[7], wrap(r - 1), c)),
    ]
    for j in range(CHUNKS):
        all_sent(j)
    for copy in started[:-2]:
        copy.wait_send()
    for copy in around:
        copy.wait_recv()

    looked = dot(pick[...], lk[...])
    lane = lax.broadcasted_iota(jnp.int32, (1, da), 1)
    masks = [((lane >= h * AHEAD) & (lane < (h + 1) * AHEAD)).astype(F32) for h in range(AHEADS)]
    w_kv = jnp.concatenate([wak[...], wav[...]], axis=1)
    w_qg = jnp.concatenate([waq[...], wag[...]], axis=1)
    root = AHEAD ** (-0.5)
    live = amask[...].astype(F32)
    ones = jnp.ones((WK, da), BF16)
    all_bias = abias[...].reshape(windows * AHEADS * WQ, WK)
    tall = AHEADS * WQ
    for s in range(samples):
        state = atom_cond + looked[:, s * da : (s + 1) * da]
        mixed = (asc[...] * layer_norm(state) + ash[...]).astype(BF16)
        kv = dot(mixed, w_kv).astype(BF16)
        own = dot(mixed[edge : edge + atoms], w_qg)
        queries = (own[:, :da] * root).astype(BF16).astype(F32)
        head_gate = jax.nn.sigmoid(own[:, da:])
        wkv = dot(windowed[...], kv).astype(BF16)
        scores = []
        for w in range(windows):
            q = queries[w * WQ : (w + 1) * WQ]
            wide_q = jnp.concatenate([q * m for m in masks], axis=0).astype(BF16)
            scores.append(dot_nt(wide_q, wkv[w * WK : (w + 1) * WK, :da]))
        scores = jnp.concatenate(scores, axis=0) + all_bias
        weights = jnp.exp(scores - jnp.max(scores, axis=-1, keepdims=True)).astype(BF16)
        parts = []
        for w in range(windows):
            wide_v = jnp.concatenate([wkv[w * WK : (w + 1) * WK, da:], ones], axis=1)
            summed = dot(weights[w * tall : (w + 1) * tall], wide_v)
            summed = summed[:, :da] / summed[:, da:]
            picked = summed[:WQ] * masks[0]
            for h in range(1, AHEADS):
                picked = picked + summed[h * WQ : (h + 1) * WQ] * masks[h]
            parts.append(picked)
        atom_gated = (head_gate * jnp.concatenate(parts, axis=0)).astype(BF16)
        final = state[edge : edge + atoms] + dot(atom_gated, wao[...])
        out[s] = dot_nt(wup[...], layer_norm(final).astype(BF16)) * live
    for copy in started[-2:]:
        copy.wait_send()


def shards(
    rows,
    tokens_in, cond_single, token_mask, pair_cond, w_pair, w_scale, w_shift, w_outgate,
    w_query, w_key, w_value, w_gate, w_out, atom_cond, atom_token, window_start, atom_mask,
    atom_pair, w_token_atom, w_ascale, w_ashift, w_aquery, w_akey, w_avalue, w_agate, w_aout,
    w_apair, w_update,
):
    samples, toks, width = tokens_in.shape
    half = pair_cond.shape[1]
    total = 2 * half
    heads = w_pair.shape[1] // 2
    columns = w_query.shape[1]
    atoms, da = atom_cond.shape
    n = rows // 2
    hops = 2 * (n - 1)
    windows = atoms // WQ
    vmem = pl.BlockSpec(memory_space=pltpu.VMEM)
    smem = pl.BlockSpec(memory_space=pltpu.SMEM)
    anywhere = pl.BlockSpec(memory_space=pl.ANY)
    dma = pltpu.SemaphoreType.DMA
    flops = 2 * samples * total * width * columns * 4
    large = (
        tokens_in, w_scale, w_shift, pair_cond, w_query, w_gate, w_out, w_outgate, w_key, w_value,
        w_token_atom, atom_pair,
    )
    tokens_out, atom_update = pl.pallas_call(
        functools.partial(step_kernel, rows),
        name="sampler_step",
        out_shape=(
            jax.ShapeDtypeStruct((samples, toks, width), BF16),
            jax.ShapeDtypeStruct((samples, 3, atoms), F32),
        ),
        in_specs=[vmem] * 6 + [smem] * 2 + [vmem] * 8 + [anywhere] * len(large),
        out_specs=[vmem] * 2,
        scratch_shapes=[pltpu.VMEM(a.shape, a.dtype) for a in large]
        + [
            pltpu.VMEM((rows, samples, toks, width), BF16),
            pltpu.VMEM((samples, toks, columns), F32),
            pltpu.VMEM((samples, toks, columns), F32),
            pltpu.VMEM((toks, width), F32),
            pltpu.VMEM((samples, toks, columns), BF16),
            pltpu.VMEM((samples, toks, columns), BF16),
            pltpu.VMEM((columns, width), BF16),
            pltpu.VMEM((2, toks * heads, half), F32),
            pltpu.VMEM((2, toks * heads, half), F32),
            pltpu.VMEM((toks * heads, total), F32),
            pltpu.VMEM((rows, 8, total), F32),
            pltpu.VMEM((3 * toks, samples * da), BF16),
            pltpu.VMEM((atoms + WK, da), BF16),
            pltpu.VMEM((3, 8, atoms), F32),
            pltpu.VMEM((atoms + WK, da), F32),
            pltpu.VMEM((atoms + WK, da), F32),
            pltpu.VMEM((atoms + WK, 3 * toks), BF16),
            pltpu.VMEM((windows * WK, atoms + WK), BF16),
            pltpu.VMEM((windows, AHEADS * WQ, WK), F32),
            dma((len(large),)),
            dma((CHUNKS, hops)),
            dma((CHUNKS, hops)),
            dma((CHUNKS, hops + 1)),
            dma((CHUNKS, hops + 1)),
            dma((CHUNKS, 2 * hops + 1)),
            dma((CHUNKS, 2 * hops + 1)),
            dma((rows - 1,)),
            dma((rows - 1,)),
            dma((2 * CHUNKS,)),
            dma((2 * CHUNKS,)),
            dma((8,)),
            dma((8,)),
        ],
        compiler_params=pltpu.CompilerParams(
            collective_id=0, has_side_effects=True, vmem_limit_bytes=56 * 2**20
        ),
        cost_estimate=pl.CostEstimate(
            flops=flops, bytes_accessed=12 * 2**20, transcendentals=8 * 2**20
        ),
    )(
        cond_single, token_mask.reshape(1, toks), w_pair.T, atom_cond, atom_token.reshape(1, atoms),
        atom_mask.reshape(1, atoms), window_start, w_apair.astype(F32).reshape(-1), w_ascale,
        w_ashift, w_aquery, w_akey, w_avalue, w_agate, w_aout, w_update, *large,
    )
    return (tokens_out, atom_update)


def solution(mesh):
    return jax.shard_map(
        functools.partial(shards, mesh.shape["row"]),
        mesh=mesh,
        in_specs=(
            P("groups", "row", None),
            P(("groups", "row"), None),
            P(("groups", "row")),
            P(("groups", "row"), "col", None),
            P(),
            P(),
            P(),
            P(),
            P(None, "col"),
            P(None, "col"),
            P(None, "col"),
            P(None, "col"),
            P("col", None),
            P(("groups", "row", "col"), None),
            P(("groups", "row", "col")),
            P(("groups", "row", "col")),
            P(("groups", "row", "col")),
            P(("groups", "row", "col"), None, None, None),
            P(),
            P(),
            P(),
            P(),
            P(),
            P(),
            P(),
            P(),
            P(),
            P(),
        ),
        out_specs=(P("groups", "row", None), P("groups", None, ("row", "col"))),
        check_vma=False,
    )
```

```python
import functools

import jax
import jax.numpy as jnp
from jax import lax
from jax.experimental import pallas as pl
from jax.experimental.pallas import tpu as pltpu
from jax.sharding import PartitionSpec as P

HEAD = 48
AHEADS = 4
AHEAD = 32
WQ = 32
WK = 128
F32 = jnp.float32
BF16 = jnp.bfloat16


def layer_norm(inputs):
    inputs = inputs.astype(F32)
    centred = inputs - jnp.mean(inputs, axis=-1, keepdims=True)
    variance = jnp.mean(centred * centred, axis=-1, keepdims=True)
    return centred * lax.rsqrt(variance + 1e-05)


def dot(a, b):
    return jnp.dot(a, b, preferred_element_type=F32)


def dot_nt(a, b):
    return lax.dot_general(a, b, (((1,), (1,)), ((), ())), preferred_element_type=F32)


def remote(src, dst, send, recv, row, col):
    return pltpu.make_async_remote_copy(
        src_ref=src,
        dst_ref=dst,
        send_sem=send,
        recv_sem=recv,
        device_id={"row": row, "col": col},
        device_id_type=pl.DeviceIdType.MESH,
    )


def step_kernel(
    rows,
    cond, tmask, wpt, acond, atok, amask, start, wap, wasc, wash, waq, wak, wav, wag, wao, wup,
    tin_h, wsc_h, wsh_h, pc_h, wq_h, wg_h, wo_h, wog_h, wk_h, wv_h, wta_h, apair_h,
    tout, out,
    tin, wsc, wsh, pc, wq, wg, wo, wog, wk, wv, wta, apair,
    mx, mstage, qb, gate, og, gtmp, gall, wosib, pbs, bias, bfull, mk, lk, ac, tk,
    asc, ash, pick, windowed, abias,
    ls, zs, zr, cs, cr, ms, mr, gs, gr, xs, xr,
):
    r = lax.axis_index("row")
    c = lax.axis_index("col")
    other = 1 - c
    samples, toks, width = tin.shape
    heads = wpt.shape[0] // 2
    half = pc.shape[1]
    total = half * 2
    n = rows // 2
    i = r // 2
    y = r % 2
    hs = samples // 2
    per = hs // 2
    partner = i * 2 + 1 - y
    inv_root = HEAD ** (-0.5)

    def wrap(v):
        return lax.rem(v + rows, rows)

    left_row, right_row = wrap(r + c - 1), wrap(r + c)

    pairs = [
        (tin_h, tin), (wsc_h, wsc), (wsh_h, wsh), (pc_h, pc), (wq_h, wq), (wg_h, wg), (wo_h, wo),
        (wog_h, wog), (wk_h, wk), (wv_h, wv), (wta_h, wta), (apair_h, apair),
    ]
    loads = [pltpu.make_async_copy(src, dst, ls.at[k]) for k, (src, dst) in enumerate(pairs)]
    for load in loads[:3]:
        load.start()

    barrier = pltpu.get_barrier_semaphore()

    def greet(row, col):
        pl.semaphore_signal(
            barrier, inc=1, device_id={"row": row, "col": col},
            device_id_type=pl.DeviceIdType.MESH,
        )

    for d in range(1, rows):
        greet(wrap(r + d), c)
    greet(r, other)
    greet(partner, other)
    greet(wrap(r + 2 * c - 1), other)

    cond_norm = layer_norm(cond[...]).astype(BF16)
    for load in loads[:3]:
        load.wait()
    for load in loads[3:]:
        load.start()
    scale = jax.nn.sigmoid(dot(cond_norm, wsc[...]))
    shift = dot(cond_norm, wsh[...])
    for s in range(samples):
        mstage[s] = (scale * layer_norm(tin[s]) + shift).astype(BF16)
    pl.semaphore_wait(barrier, rows + 2)

    started = []

    def go(copy):
        copy.start()
        started.append(copy)
        return copy

    spots = [(e, w) for e in range(n) for w in (0, 1)][1:]

    def row_at(e, w):
        return lax.rem(i + n + e, n) * 2 + (1 - y if w else y)

    def send_own(j, k):
        e, w = spots[k]
        theirs = (1 - y if w else y) * hs + c * per + j
        go(
            remote(
                mstage.at[theirs], mx.at[r, c * per + j], zs.at[j, k], zr.at[j, k], row_at(e, w), c
            )
        )

    def core_copy(j, k, core):
        e, w = spots[k]
        ref = mx.at[row_at(-e, w), core * per + j]
        return remote(ref, ref, cs.at[j, k], cr.at[j, k], r, other)

    def forward(j, k):
        e, w = spots[k]
        src = row_at(-e, w)
        ref = mx.at[src, c * per + j]
        remote(ref, ref, zs.at[j, k], zr.at[j, k], src, c).wait_recv()
        go(core_copy(j, k, c))

    far = range(1, len(spots))
    for j in range(per):
        send_own(j, 0)
    for k in far:
        send_own(0, k)
    mx[r] = mstage[pl.ds(y * hs, hs)]

    placed = (
        lax.broadcasted_iota(jnp.int32, (toks, total), 1)
        == lax.broadcasted_iota(jnp.int32, (toks, total), 0) + r * toks
    ).astype(F32)
    present = jnp.broadcast_to(tmask[...], (8, toks)).astype(F32)
    mk[r] = dot(present, placed)
    for d in range(1, rows):
        go(remote(mk.at[r], mk.at[r], ms.at[d - 1], mr.at[d - 1], wrap(r + d), c))
    tk[1] = jnp.broadcast_to(atok[...], (8, atok.shape[1])).astype(F32)
    edge = WK // 2
    atoms = acond.shape[0]
    ac[edge : edge + atoms] = acond[...]
    edges = [
        go(remote(tk.at[1], tk.at[0], xs.at[1], xr.at[1], right_row, other)),
        go(remote(tk.at[1], tk.at[2], xs.at[2], xr.at[2], left_row, other)),
        go(remote(ac.at[pl.ds(atoms, edge)], ac.at[pl.ds(0, edge)], xs.at[3], xr.at[3], right_row, other)),
        go(remote(ac.at[pl.ds(edge, edge)], ac.at[pl.ds(atoms + edge, edge)], xs.at[4], xr.at[4], left_row, other)),
    ]

    loads[3].wait()
    for q in range(toks):
        part = dot_nt(wpt[...], pc[q])
        pbs[0, q * heads : (q + 1) * heads] = part[:heads]
        pbs[1, q * heads : (q + 1) * heads] = part[heads:]
    bias_copies = [
        go(remote(pbs.at[other], bias.at[y, c], xs.at[5], xr.at[5], r, other)),
        go(remote(pbs.at[c], bias.at[y, c], xs.at[8], xr.at[8], partner, c)),
        go(remote(pbs.at[other], bias.at[y, c], xs.at[9], xr.at[9], partner, other)),
    ]
    bias[y, c] = pbs[c]
    for j in range(per):
        forward(j, 0)
    for j in range(1, per):
        for k in far:
            send_own(j, k)

    for load in loads[4:7]:
        load.wait()
    wide_out = go(remote(wo, wosib, xs.at[0], xr.at[0], r, other))
    loads[7].wait()
    og[...] = jax.nn.sigmoid(dot(cond_norm, wog[...]))

    for copy in edges:
        copy.wait_recv()
    da = ac.shape[1]
    span = ac.shape[0]
    windows = atoms // WQ
    near = lk.shape[0]
    atom_cond = ac[...].astype(F32)
    atom_norm = layer_norm(atom_cond).astype(BF16)
    asc[...] = jax.nn.sigmoid(dot(atom_norm, wasc[...]))
    ash[...] = dot(atom_norm, wash[...])
    cols = [jnp.transpose(tk[k])[:, 0:1] for k in range(3)]
    token = jnp.concatenate([cols[0][atoms - edge :], cols[1], cols[2][:edge]], axis=0)
    token = token - (r * toks - toks).astype(F32)
    pick[...] = (
        token == lax.broadcasted_iota(jnp.int32, (span, near), 1).astype(F32)
    ).astype(BF16)
    base = (r * 2 + c) * atoms - edge
    place = lax.broadcasted_iota(jnp.int32, (WK, span), 1) - lax.broadcasted_iota(
        jnp.int32, (WK, span), 0
    )
    for w in range(windows):
        windowed[w * WK : (w + 1) * WK] = (place == start[w] - base).astype(F32).astype(BF16)
    loads[11].wait()
    wap_f = wap[...].astype(F32)
    for h in range(AHEADS):
        acc = apair[:, 0].astype(F32) * wap_f[h : h + 1, 0:1]
        for ch in range(1, apair.shape[1]):
            acc = acc + apair[:, ch].astype(F32) * wap_f[h : h + 1, ch : ch + 1]
        abias[:, h * WQ : (h + 1) * WQ] = acc

    for j in range(per):
        core_copy(j, 0, other).wait_recv()
    both = mx[pl.ds(2 * i, 2)].reshape(2 * hs * toks, width)
    qb[...] = (dot(both, wq[...]) * inv_root).astype(BF16).astype(F32).reshape(qb.shape)
    gate[...] = jax.nn.sigmoid(dot(both, wg[...])).reshape(gate.shape)

    columns = wq.shape[1]
    lane = lax.broadcasted_iota(jnp.int32, (heads, columns), 1)
    first = lax.broadcasted_iota(jnp.int32, (heads, columns), 0) * HEAD
    head_mask = ((lane >= first) & (lane < first + HEAD)).astype(F32)

    def attend(s, carry):
        keys_in = mx[:, s].reshape(total, width)
        keys = dot(keys_in, wk[...]).astype(BF16)
        values = dot(keys_in, wv[...]).astype(BF16)
        values = jnp.concatenate([values, jnp.ones((total, 128), BF16)], axis=1)
        wide_q = qb[:, s].reshape(2 * toks, 1, columns) * head_mask[None]
        wide_q = wide_q.reshape(2 * toks * heads, columns).astype(BF16)
        scores = dot_nt(wide_q, keys) + bfull[...]
        weights = jnp.exp(scores - jnp.max(scores, axis=-1, keepdims=True))
        summed = dot(weights.astype(BF16), values)
        inverse = 1.0 / summed[:, columns:]
        summed = summed[:, :columns] * jnp.concatenate([inverse] * (columns // 128), axis=1)
        picked = summed.reshape(2 * toks, heads, columns) * head_mask[None]
        attended = jnp.sum(picked, axis=1).reshape(2, toks, columns)
        gtmp[:, s] = (gate[:, s] * attended).astype(BF16)
        return carry

    for d in range(1, rows):
        slot = mk.at[wrap(r - d)]
        remote(slot, slot, ms.at[d - 1], mr.at[d - 1], r, other).wait_recv()
    for copy in bias_copies:
        copy.wait_recv()
    shift_row = (jnp.sum(mk[...], axis=0) - 1.0)[0:1] * 10000.0
    for q in range(2):
        for k in range(2):
            cut = slice(k * half, (k + 1) * half)
            tall = slice(q * toks * heads, (q + 1) * toks * heads)
            bfull[tall, cut] = bias[q, k] + shift_row[:, cut]
    loads[8].wait()
    loads[9].wait()
    gated_copies = []

    for j in range(per):
        for k in far:
            forward(j, k)
        for k in far:
            core_copy(j, k, other).wait_recv()
        lax.fori_loop(0, 2, lambda core, carry: attend(core * per + j, carry), None)
        for core in range(2):
            s = core * per + j
            dst = gall.at[c, y * hs + s]
            gated_copies.append(go(remote(gtmp.at[1 - y, s], dst, gs.at[0, s], gr.at[0, s], partner, c)))
            gated_copies.append(go(remote(gtmp.at[1 - y, s], dst, gs.at[1, s], gr.at[1, s], partner, other)))
            gated_copies.append(go(remote(gtmp.at[y, s], dst, gs.at[2, s], gr.at[2, s], r, other)))
            gall[c, y * hs + s] = gtmp[y, s]

    wide_out.wait_recv()
    loads[10].wait()
    for copy in gated_copies:
        copy.wait_recv()
    update = dot(gall[c].reshape(samples * toks, columns), wo[...]) + dot(
        gall[other].reshape(samples * toks, columns), wosib[...]
    )
    for s in range(samples):
        tokens = (tin[s].astype(F32) + og[...] * update[s * toks : (s + 1) * toks]).astype(BF16)
        tout[s] = tokens
        proj = dot(layer_norm(tokens).astype(BF16), wta[...]).astype(BF16)
        lk[toks : 2 * toks, s * da : (s + 1) * da] = proj
    mine = lk.at[pl.ds(toks, toks)]
    around = [
        go(remote(mine, lk.at[pl.ds(0, toks)], xs.at[6], xr.at[6], wrap(r + 1), c)),
        go(remote(mine, lk.at[pl.ds(2 * toks, toks)], xs.at[7], xr.at[7], wrap(r - 1), c)),
    ]
    for copy in started[:-2]:
        copy.wait_send()
    for copy in around:
        copy.wait_recv()

    looked = dot(pick[...], lk[...])
    lane = lax.broadcasted_iota(jnp.int32, (1, da), 1)
    masks = [((lane >= h * AHEAD) & (lane < (h + 1) * AHEAD)).astype(F32) for h in range(AHEADS)]
    w_kv = jnp.concatenate([wak[...], wav[...]], axis=1)
    w_qg = jnp.concatenate([waq[...], wag[...]], axis=1)
    root = AHEAD ** (-0.5)
    live = amask[...].astype(F32)
    ones = jnp.ones((WK, da), BF16)
    all_bias = abias[...].reshape(windows * AHEADS * WQ, WK)
    tall = AHEADS * WQ
    for s in range(samples):
        state = atom_cond + looked[:, s * da : (s + 1) * da]
        mixed = (asc[...] * layer_norm(state) + ash[...]).astype(BF16)
        kv = dot(mixed, w_kv).astype(BF16)
        own = dot(mixed[edge : edge + atoms], w_qg)
        queries = (own[:, :da] * root).astype(BF16).astype(F32)
        head_gate = jax.nn.sigmoid(own[:, da:])
        wkv = dot(windowed[...], kv).astype(BF16)
        scores = []
        for w in range(windows):
            q = queries[w * WQ : (w + 1) * WQ]
            wide_q = jnp.concatenate([q * m for m in masks], axis=0).astype(BF16)
            scores.append(dot_nt(wide_q, wkv[w * WK : (w + 1) * WK, :da]))
        scores = jnp.concatenate(scores, axis=0) + all_bias
        weights = jnp.exp(scores - jnp.max(scores, axis=-1, keepdims=True)).astype(BF16)
        parts = []
        for w in range(windows):
            wide_v = jnp.concatenate([wkv[w * WK : (w + 1) * WK, da:], ones], axis=1)
            summed = dot(weights[w * tall : (w + 1) * tall], wide_v)
            summed = summed[:, :da] / summed[:, da:]
            picked = summed[:WQ] * masks[0]
            for h in range(1, AHEADS):
                picked = picked + summed[h * WQ : (h + 1) * WQ] * masks[h]
            parts.append(picked)
        atom_gated = (head_gate * jnp.concatenate(parts, axis=0)).astype(BF16)
        final = state[edge : edge + atoms] + dot(atom_gated, wao[...])
        moved = dot_nt(wup[...], layer_norm(final).astype(BF16)) * live
        for axis in range(moved.shape[0]):
            out[axis, s : s + 1] = moved[axis : axis + 1]
    for copy in started[-2:]:
        copy.wait_send()


def shards(
    rows,
    tokens_in, cond_single, token_mask, pair_cond, w_pair, w_scale, w_shift, w_outgate,
    w_query, w_key, w_value, w_gate, w_out, atom_cond, atom_token, window_start, atom_mask,
    atom_pair, w_token_atom, w_ascale, w_ashift, w_aquery, w_akey, w_avalue, w_agate, w_aout,
    w_apair, w_update,
):
    samples, toks, width = tokens_in.shape
    half = pair_cond.shape[1]
    total = 2 * half
    heads = w_pair.shape[1] // 2
    columns = w_query.shape[1]
    atoms, da = atom_cond.shape
    hs = samples // 2
    per = hs // 2
    windows = atoms // WQ
    vmem = pl.BlockSpec(memory_space=pltpu.VMEM)
    smem = pl.BlockSpec(memory_space=pltpu.SMEM)
    anywhere = pl.BlockSpec(memory_space=pl.ANY)
    dma = pltpu.SemaphoreType.DMA
    flops = 2 * samples * total * width * columns * 4
    large = (
        tokens_in, w_scale, w_shift, pair_cond, w_query, w_gate, w_out, w_outgate, w_key, w_value,
        w_token_atom, atom_pair,
    )
    tokens_out, atom_update = pl.pallas_call(
        functools.partial(step_kernel, rows),
        name="sampler_step",
        out_shape=(
            jax.ShapeDtypeStruct((samples, toks, width), BF16),
            jax.ShapeDtypeStruct((3, samples, atoms), F32),
        ),
        in_specs=[vmem] * 6 + [smem] + [vmem] * 9 + [anywhere] * len(large),
        out_specs=[vmem] * 2,
        scratch_shapes=[pltpu.VMEM(a.shape, a.dtype) for a in large]
        + [
            pltpu.VMEM((rows, hs, toks, width), BF16),
            pltpu.VMEM((samples, toks, width), BF16),
            pltpu.VMEM((2, hs, toks, columns), F32),
            pltpu.VMEM((2, hs, toks, columns), F32),
            pltpu.VMEM((toks, width), F32),
            pltpu.VMEM((2, hs, toks, columns), BF16),
            pltpu.VMEM((2, samples, toks, columns), BF16),
            pltpu.VMEM((columns, width), BF16),
            pltpu.VMEM((2, toks * heads, half), F32),
            pltpu.VMEM((2, 2, toks * heads, half), F32),
            pltpu.VMEM((2 * toks * heads, total), F32),
            pltpu.VMEM((rows, 8, total), F32),
            pltpu.VMEM((3 * toks, samples * da), BF16),
            pltpu.VMEM((atoms + WK, da), BF16),
            pltpu.VMEM((3, 8, atoms), F32),
            pltpu.VMEM((atoms + WK, da), F32),
            pltpu.VMEM((atoms + WK, da), F32),
            pltpu.VMEM((atoms + WK, 3 * toks), BF16),
            pltpu.VMEM((windows * WK, atoms + WK), BF16),
            pltpu.VMEM((windows, AHEADS * WQ, WK), F32),
            dma((len(large),)),
            dma((per, rows - 1)),
            dma((per, rows - 1)),
            dma((per, rows - 1)),
            dma((per, rows - 1)),
            dma((rows - 1,)),
            dma((rows - 1,)),
            dma((3, hs)),
            dma((3, hs)),
            dma((10,)),
            dma((10,)),
        ],
        compiler_params=pltpu.CompilerParams(
            collective_id=0, has_side_effects=True, vmem_limit_bytes=56 * 2**20
        ),
        cost_estimate=pl.CostEstimate(
            flops=flops, bytes_accessed=12 * 2**20, transcendentals=8 * 2**20
        ),
    )(
        cond_single, token_mask.reshape(1, toks), w_pair.T, atom_cond, atom_token.reshape(1, atoms),
        atom_mask.reshape(1, atoms), window_start, w_apair.T, w_ascale,
        w_ashift, w_aquery, w_akey, w_avalue, w_agate, w_aout, w_update, *large,
    )
    return (tokens_out, jnp.transpose(atom_update, (1, 0, 2)))


def solution(mesh):
    return jax.shard_map(
        functools.partial(shards, mesh.shape["row"]),
        mesh=mesh,
        in_specs=(
            P("groups", "row", None),
            P(("groups", "row"), None),
            P(("groups", "row")),
            P(("groups", "row"), "col", None),
            P(),
            P(),
            P(),
            P(),
            P(None, "col"),
            P(None, "col"),
            P(None, "col"),
            P(None, "col"),
            P("col", None),
            P(("groups", "row", "col"), None),
            P(("groups", "row", "col")),
            P(("groups", "row", "col")),
            P(("groups", "row", "col")),
            P(("groups", "row", "col"), None, None, None),
            P(),
            P(),
            P(),
            P(),
            P(),
            P(),
            P(),
            P(),
            P(),
            P(),
        ),
        out_specs=(P("groups", "row", None), P("groups", None, ("row", "col"))),
        check_vma=False,
    )
```

```python
import functools

import jax
import jax.numpy as jnp
from jax import lax
from jax.experimental import pallas as pl
from jax.experimental.pallas import tpu as pltpu
from jax.sharding import PartitionSpec as P

HEAD = 48
AHEADS = 4
AHEAD = 32
WQ = 32
WK = 128
F32 = jnp.float32
BF16 = jnp.bfloat16


def layer_norm(inputs):
    inputs = inputs.astype(F32)
    centred = inputs - jnp.mean(inputs, axis=-1, keepdims=True)
    variance = jnp.mean(centred * centred, axis=-1, keepdims=True)
    return centred * lax.rsqrt(variance + 1e-05)


def dot(a, b):
    return jnp.dot(a, b, preferred_element_type=F32)


def dot_nt(a, b):
    return lax.dot_general(a, b, (((1,), (1,)), ((), ())), preferred_element_type=F32)


def remote(src, dst, send, recv, row, col):
    return pltpu.make_async_remote_copy(
        src_ref=src,
        dst_ref=dst,
        send_sem=send,
        recv_sem=recv,
        device_id={"row": row, "col": col},
        device_id_type=pl.DeviceIdType.MESH,
    )


def step_kernel(
    rows,
    cond, tmask, wpt, acond, atok, amask, start, wap, wasc, wash, waq, wak, wav, wag, wao, wup,
    tin_h, wsc_h, wsh_h, pc_h, wq_h, wg_h, wo_h, wog_h, wk_h, wv_h, wta_h, apair_h,
    tout, out,
    tin, wsc, wsh, pc, wq, wg, wo, wog, wk, wv, wta, apair,
    mx, mstage, qb, gate, og, gtmp, gall, wosib, pbs, bias, bfull, mk, lk, ac, tk,
    asc, ash, pick, windowed, abias,
    ls, zs, zr, cs, cr, ms, mr, gs, gr, xs, xr,
):
    r = lax.axis_index("row")
    c = lax.axis_index("col")
    other = 1 - c
    samples, toks, width = tin.shape
    heads = wpt.shape[0] // 2
    half = pc.shape[1]
    total = half * 2
    n = rows // 2
    i = r // 2
    y = r % 2
    hs = samples // 2
    per = hs // 2
    partner = i * 2 + 1 - y
    inv_root = HEAD ** (-0.5)

    def wrap(v):
        return lax.rem(v + rows, rows)

    left_row, right_row = wrap(r + c - 1), wrap(r + c)

    pairs = [
        (tin_h, tin), (wsc_h, wsc), (wsh_h, wsh), (pc_h, pc), (wq_h, wq), (wg_h, wg), (wo_h, wo),
        (wog_h, wog), (wk_h, wk), (wv_h, wv), (wta_h, wta), (apair_h, apair),
    ]
    loads = [pltpu.make_async_copy(src, dst, ls.at[k]) for k, (src, dst) in enumerate(pairs)]
    for load in loads[:3]:
        load.start()

    barrier = pltpu.get_barrier_semaphore()

    def greet(row, col):
        pl.semaphore_signal(
            barrier, inc=1, device_id={"row": row, "col": col},
            device_id_type=pl.DeviceIdType.MESH,
        )

    for d in range(1, rows):
        greet(wrap(r + d), c)
    greet(r, other)
    greet(partner, other)
    greet(wrap(r + 2 * c - 1), other)

    cond_norm = layer_norm(cond[...]).astype(BF16)
    for load in loads[:3]:
        load.wait()
    for load in loads[3:]:
        load.start()
    scale = jax.nn.sigmoid(dot(cond_norm, wsc[...]))
    shift = dot(cond_norm, wsh[...])

    def mix(s):
        return (scale * layer_norm(tin[s]) + shift).astype(BF16)

    for side in range(2):
        mstage[side * hs + c * per] = mix(side * hs + c * per)
    pl.semaphore_wait(barrier, rows + 2)

    started = []

    def go(copy):
        copy.start()
        started.append(copy)
        return copy

    spots = [(e, w) for e in range(n) for w in (0, 1)][1:]

    def row_at(e, w):
        return lax.rem(i + n + e, n) * 2 + (1 - y if w else y)

    def send_own(j, k):
        e, w = spots[k]
        theirs = (1 - y if w else y) * hs + c * per + j
        go(
            remote(
                mstage.at[theirs], mx.at[r, c * per + j], zs.at[j, k], zr.at[j, k], row_at(e, w), c
            )
        )

    def core_copy(j, k, core):
        e, w = spots[k]
        ref = mx.at[row_at(-e, w), core * per + j]
        return remote(ref, ref, cs.at[j, k], cr.at[j, k], r, other)

    def forward(j, k):
        e, w = spots[k]
        src = row_at(-e, w)
        ref = mx.at[src, c * per + j]
        remote(ref, ref, zs.at[j, k], zr.at[j, k], src, c).wait_recv()
        go(core_copy(j, k, c))

    far = range(1, len(spots))
    send_own(0, 0)
    for k in far:
        send_own(0, k)
    for j in range(1, per):
        for side in range(2):
            mstage[side * hs + c * per + j] = mix(side * hs + c * per + j)
        send_own(j, 0)
    for j in range(per):
        mx[r, c * per + j] = mstage[y * hs + c * per + j]
        mx[r, other * per + j] = mix(y * hs + other * per + j)

    placed = (
        lax.broadcasted_iota(jnp.int32, (toks, total), 1)
        == lax.broadcasted_iota(jnp.int32, (toks, total), 0) + r * toks
    ).astype(F32)
    present = jnp.broadcast_to(tmask[...], (8, toks)).astype(F32)
    mk[r] = dot(present, placed)
    for d in range(1, rows):
        go(remote(mk.at[r], mk.at[r], ms.at[d - 1], mr.at[d - 1], wrap(r + d), c))
    tk[1] = jnp.broadcast_to(atok[...], (8, atok.shape[1])).astype(F32)
    edge = WK // 2
    atoms = acond.shape[0]
    ac[edge : edge + atoms] = acond[...]
    edges = [
        go(remote(tk.at[1], tk.at[0], xs.at[1], xr.at[1], right_row, other)),
        go(remote(tk.at[1], tk.at[2], xs.at[2], xr.at[2], left_row, other)),
        go(remote(ac.at[pl.ds(atoms, edge)], ac.at[pl.ds(0, edge)], xs.at[3], xr.at[3], right_row, other)),
        go(remote(ac.at[pl.ds(edge, edge)], ac.at[pl.ds(atoms + edge, edge)], xs.at[4], xr.at[4], left_row, other)),
    ]

    loads[3].wait()
    for q in range(toks):
        part = dot_nt(wpt[...], pc[q])
        pbs[0, q * heads : (q + 1) * heads] = part[:heads]
        pbs[1, q * heads : (q + 1) * heads] = part[heads:]
    bias_copies = [
        go(remote(pbs.at[other], bias.at[y, c], xs.at[5], xr.at[5], r, other)),
        go(remote(pbs.at[c], bias.at[y, c], xs.at[8], xr.at[8], partner, c)),
        go(remote(pbs.at[other], bias.at[y, c], xs.at[9], xr.at[9], partner, other)),
    ]
    bias[y, c] = pbs[c]
    for j in range(per):
        forward(j, 0)
    for j in range(1, per):
        for k in far:
            send_own(j, k)

    for load in loads[4:7]:
        load.wait()
    wide_out = go(remote(wo, wosib, xs.at[0], xr.at[0], r, other))
    loads[7].wait()
    og[...] = jax.nn.sigmoid(dot(cond_norm, wog[...]))

    for copy in edges:
        copy.wait_recv()
    da = ac.shape[1]
    span = ac.shape[0]
    windows = atoms // WQ
    near = lk.shape[0]
    atom_cond = ac[...].astype(F32)
    atom_norm = layer_norm(atom_cond).astype(BF16)
    asc[...] = jax.nn.sigmoid(dot(atom_norm, wasc[...]))
    ash[...] = dot(atom_norm, wash[...])
    cols = [jnp.transpose(tk[k])[:, 0:1] for k in range(3)]
    token = jnp.concatenate([cols[0][atoms - edge :], cols[1], cols[2][:edge]], axis=0)
    token = token - (r * toks - toks).astype(F32)
    pick[...] = (
        token == lax.broadcasted_iota(jnp.int32, (span, near), 1).astype(F32)
    ).astype(BF16)
    base = (r * 2 + c) * atoms - edge
    place = lax.broadcasted_iota(jnp.int32, (WK, span), 1) - lax.broadcasted_iota(
        jnp.int32, (WK, span), 0
    )
    for w in range(windows):
        windowed[w * WK : (w + 1) * WK] = (place == start[w] - base).astype(F32).astype(BF16)
    loads[11].wait()
    wap_f = wap[...].astype(F32)
    for h in range(AHEADS):
        acc = apair[:, 0].astype(F32) * wap_f[h : h + 1, 0:1]
        for ch in range(1, apair.shape[1]):
            acc = acc + apair[:, ch].astype(F32) * wap_f[h : h + 1, ch : ch + 1]
        abias[:, h * WQ : (h + 1) * WQ] = acc

    for j in range(per):
        core_copy(j, 0, other).wait_recv()
    both = mx[pl.ds(2 * i, 2)].reshape(2 * hs * toks, width)
    qb[...] = (dot(both, wq[...]) * inv_root).astype(BF16).astype(F32).reshape(qb.shape)
    gate[...] = jax.nn.sigmoid(dot(both, wg[...])).reshape(gate.shape)

    columns = wq.shape[1]
    lane = lax.broadcasted_iota(jnp.int32, (heads, columns), 1)
    first = lax.broadcasted_iota(jnp.int32, (heads, columns), 0) * HEAD
    head_mask = ((lane >= first) & (lane < first + HEAD)).astype(F32)

    def attend(s):
        keys_in = mx[:, s].reshape(total, width)
        keys = dot(keys_in, wk[...]).astype(BF16)
        values = dot(keys_in, wv[...]).astype(BF16)
        values = jnp.concatenate([values, jnp.ones((total, 128), BF16)], axis=1)
        wide_q = qb[:, s].reshape(2 * toks, 1, columns) * head_mask[None]
        wide_q = wide_q.reshape(2 * toks * heads, columns).astype(BF16)
        scores = dot_nt(wide_q, keys) + bfull[...]
        weights = jnp.exp(scores - jnp.max(scores, axis=-1, keepdims=True))
        summed = dot(weights.astype(BF16), values)
        inverse = 1.0 / summed[:, columns:]
        summed = summed[:, :columns] * jnp.concatenate([inverse] * (columns // 128), axis=1)
        picked = summed.reshape(2 * toks, heads, columns) * head_mask[None]
        attended = jnp.sum(picked, axis=1).reshape(2, toks, columns)
        gtmp[:, s] = (gate[:, s] * attended).astype(BF16)

    for d in range(1, rows):
        slot = mk.at[wrap(r - d)]
        remote(slot, slot, ms.at[d - 1], mr.at[d - 1], r, other).wait_recv()
    for copy in bias_copies:
        copy.wait_recv()
    shift_row = (jnp.sum(mk[...], axis=0) - 1.0)[0:1] * 10000.0
    for q in range(2):
        for k in range(2):
            cut = slice(k * half, (k + 1) * half)
            tall = slice(q * toks * heads, (q + 1) * toks * heads)
            bfull[tall, cut] = bias[q, k] + shift_row[:, cut]
    loads[8].wait()
    loads[9].wait()
    gated_copies = []

    for j in range(per):
        for k in far:
            forward(j, k)
        for k in far:
            core_copy(j, k, other).wait_recv()
        for core in range(2):
            attend(core * per + j)
        for core in range(2):
            s = core * per + j
            dst = gall.at[c, y * hs + s]
            gated_copies.append(go(remote(gtmp.at[1 - y, s], dst, gs.at[0, s], gr.at[0, s], partner, c)))
            gated_copies.append(go(remote(gtmp.at[1 - y, s], dst, gs.at[1, s], gr.at[1, s], partner, other)))
            gated_copies.append(go(remote(gtmp.at[y, s], dst, gs.at[2, s], gr.at[2, s], r, other)))
            gall[c, y * hs + s] = gtmp[y, s]

    wide_out.wait_recv()
    loads[10].wait()
    for copy in gated_copies:
        copy.wait_recv()
    update = dot(gall[c].reshape(samples * toks, columns), wo[...]) + dot(
        gall[other].reshape(samples * toks, columns), wosib[...]
    )
    normed = []
    for s in range(samples):
        tokens = (tin[s].astype(F32) + og[...] * update[s * toks : (s + 1) * toks]).astype(BF16)
        tout[s] = tokens
        normed.append(layer_norm(tokens).astype(BF16))
    proj = dot(jnp.concatenate(normed, axis=0), wta[...]).astype(BF16)
    for s in range(samples):
        lk[toks : 2 * toks, s * da : (s + 1) * da] = proj[s * toks : (s + 1) * toks]
    mine = lk.at[pl.ds(toks, toks)]
    around = [
        go(remote(mine, lk.at[pl.ds(0, toks)], xs.at[6], xr.at[6], wrap(r + 1), c)),
        go(remote(mine, lk.at[pl.ds(2 * toks, toks)], xs.at[7], xr.at[7], wrap(r - 1), c)),
    ]
    for copy in started[:-2]:
        copy.wait_send()
    for copy in around:
        copy.wait_recv()

    looked = dot(pick[...], lk[...])
    lane = lax.broadcasted_iota(jnp.int32, (1, da), 1)
    masks = [((lane >= h * AHEAD) & (lane < (h + 1) * AHEAD)).astype(F32) for h in range(AHEADS)]
    w_kv = jnp.concatenate([wak[...], wav[...]], axis=1)
    w_qg = jnp.concatenate([waq[...], wag[...]], axis=1)
    root = AHEAD ** (-0.5)
    live = amask[...].astype(F32)
    ones = jnp.ones((WK, da), BF16)
    all_bias = abias[...].reshape(windows * AHEADS * WQ, WK)
    tall = AHEADS * WQ
    states, mixes = [], []
    for s in range(samples):
        state = atom_cond + looked[:, s * da : (s + 1) * da]
        states.append(state[edge : edge + atoms])
        mixes.append((asc[...] * layer_norm(state) + ash[...]).astype(BF16))
    kv = dot(jnp.concatenate(mixes, axis=0), w_kv).astype(BF16)
    own = dot(jnp.concatenate([m[edge : edge + atoms] for m in mixes], axis=0), w_qg)
    queries = (own[:, :da] * root).astype(BF16).astype(F32)
    head_gate = jax.nn.sigmoid(own[:, da:])
    wkv = [dot(windowed[...], kv[s * span : (s + 1) * span]).astype(BF16) for s in range(samples)]
    scores = []
    for s in range(samples):
        for w in range(windows):
            q = queries[s * atoms + w * WQ : s * atoms + (w + 1) * WQ]
            wide_q = jnp.concatenate([q * m for m in masks], axis=0).astype(BF16)
            scores.append(
                dot_nt(wide_q, wkv[s][w * WK : (w + 1) * WK, :da])
                + all_bias[w * tall : (w + 1) * tall]
            )
    weights = [
        jnp.exp(score - jnp.max(score, axis=-1, keepdims=True)).astype(BF16) for score in scores
    ]
    parts = []
    for s in range(samples):
        for w in range(windows):
            wide_v = jnp.concatenate([wkv[s][w * WK : (w + 1) * WK, da:], ones], axis=1)
            summed = dot(weights[s * windows + w], wide_v)
            summed = summed[:, :da] / summed[:, da:]
            picked = summed[:WQ] * masks[0]
            for h in range(1, AHEADS):
                picked = picked + summed[h * WQ : (h + 1) * WQ] * masks[h]
            parts.append(picked)
    atom_gated = (head_gate * jnp.concatenate(parts, axis=0)).astype(BF16)
    final = jnp.concatenate(states, axis=0) + dot(atom_gated, wao[...])
    moved = dot_nt(wup[...], layer_norm(final).astype(BF16))
    for s in range(samples):
        for axis in range(moved.shape[0]):
            out[axis, s : s + 1] = moved[axis : axis + 1, s * atoms : (s + 1) * atoms] * live
    for copy in started[-2:]:
        copy.wait_send()


def shards(
    rows,
    tokens_in, cond_single, token_mask, pair_cond, w_pair, w_scale, w_shift, w_outgate,
    w_query, w_key, w_value, w_gate, w_out, atom_cond, atom_token, window_start, atom_mask,
    atom_pair, w_token_atom, w_ascale, w_ashift, w_aquery, w_akey, w_avalue, w_agate, w_aout,
    w_apair, w_update,
):
    samples, toks, width = tokens_in.shape
    half = pair_cond.shape[1]
    total = 2 * half
    heads = w_pair.shape[1] // 2
    columns = w_query.shape[1]
    atoms, da = atom_cond.shape
    hs = samples // 2
    per = hs // 2
    windows = atoms // WQ
    vmem = pl.BlockSpec(memory_space=pltpu.VMEM)
    smem = pl.BlockSpec(memory_space=pltpu.SMEM)
    anywhere = pl.BlockSpec(memory_space=pl.ANY)
    dma = pltpu.SemaphoreType.DMA
    flops = 2 * samples * total * width * columns * 4
    large = (
        tokens_in, w_scale, w_shift, pair_cond, w_query, w_gate, w_out, w_outgate, w_key, w_value,
        w_token_atom, atom_pair,
    )
    tokens_out, atom_update = pl.pallas_call(
        functools.partial(step_kernel, rows),
        name="sampler_step",
        out_shape=(
            jax.ShapeDtypeStruct((samples, toks, width), BF16),
            jax.ShapeDtypeStruct((3, samples, atoms), F32),
        ),
        in_specs=[vmem] * 6 + [smem] + [vmem] * 9 + [anywhere] * len(large),
        out_specs=[vmem] * 2,
        scratch_shapes=[pltpu.VMEM(a.shape, a.dtype) for a in large]
        + [
            pltpu.VMEM((rows, hs, toks, width), BF16),
            pltpu.VMEM((samples, toks, width), BF16),
            pltpu.VMEM((2, hs, toks, columns), F32),
            pltpu.VMEM((2, hs, toks, columns), F32),
            pltpu.VMEM((toks, width), F32),
            pltpu.VMEM((2, hs, toks, columns), BF16),
            pltpu.VMEM((2, samples, toks, columns), BF16),
            pltpu.VMEM((columns, width), BF16),
            pltpu.VMEM((2, toks * heads, half), F32),
            pltpu.VMEM((2, 2, toks * heads, half), F32),
            pltpu.VMEM((2 * toks * heads, total), F32),
            pltpu.VMEM((rows, 8, total), F32),
            pltpu.VMEM((3 * toks, samples * da), BF16),
            pltpu.VMEM((atoms + WK, da), BF16),
            pltpu.VMEM((3, 8, atoms), F32),
            pltpu.VMEM((atoms + WK, da), F32),
            pltpu.VMEM((atoms + WK, da), F32),
            pltpu.VMEM((atoms + WK, 3 * toks), BF16),
            pltpu.VMEM((windows * WK, atoms + WK), BF16),
            pltpu.VMEM((windows, AHEADS * WQ, WK), F32),
            dma((len(large),)),
            dma((per, rows - 1)),
            dma((per, rows - 1)),
            dma((per, rows - 1)),
            dma((per, rows - 1)),
            dma((rows - 1,)),
            dma((rows - 1,)),
            dma((3, hs)),
            dma((3, hs)),
            dma((10,)),
            dma((10,)),
        ],
        compiler_params=pltpu.CompilerParams(
            collective_id=0, has_side_effects=True, vmem_limit_bytes=56 * 2**20
        ),
        cost_estimate=pl.CostEstimate(
            flops=flops, bytes_accessed=12 * 2**20, transcendentals=8 * 2**20
        ),
    )(
        cond_single, token_mask.reshape(1, toks), w_pair.T, atom_cond, atom_token.reshape(1, atoms),
        atom_mask.reshape(1, atoms), window_start, w_apair.T, w_ascale,
        w_ashift, w_aquery, w_akey, w_avalue, w_agate, w_aout, w_update, *large,
    )
    return (tokens_out, jnp.transpose(atom_update, (1, 0, 2)))


def solution(mesh):
    return jax.shard_map(
        functools.partial(shards, mesh.shape["row"]),
        mesh=mesh,
        in_specs=(
            P("groups", "row", None),
            P(("groups", "row"), None),
            P(("groups", "row")),
            P(("groups", "row"), "col", None),
            P(),
            P(),
            P(),
            P(),
            P(None, "col"),
            P(None, "col"),
            P(None, "col"),
            P(None, "col"),
            P("col", None),
            P(("groups", "row", "col"), None),
            P(("groups", "row", "col")),
            P(("groups", "row", "col")),
            P(("groups", "row", "col")),
            P(("groups", "row", "col"), None, None, None),
            P(),
            P(),
            P(),
            P(),
            P(),
            P(),
            P(),
            P(),
            P(),
            P(),
        ),
        out_specs=(P("groups", "row", None), P("groups", None, ("row", "col"))),
        check_vma=False,
    )
```
